512 devices in a mesh: grid: 128 (over z, y, core), band: 4 (over x).
Axes of the slice: x: 4, y: 8, z: 8, core: 2. Of those that a mesh axis runs over, the one named last changes fastest.
Arguments:
- visibility: float32 [4, 16384, 2, 384], P('band', 'grid'), may hold values from -6 to 6
- weights: float32 [4, 16384, 384], P('band', 'grid'), may hold values from 0.2 to 2
- block_uv: float32 [16384, 2, 16], P('grid'), may hold values from -19 to 19
- chan_ratio: float32 [4, 24], P('band'), may hold values from 0.6 to 1
- block_subgrid: int32 [4, 16384], P('band', 'grid'), may hold values from 0 to 1023, as said below
- block_stations: int32 [16384, 2], P('grid'), may hold values from 0 to 127, as said below
- screens: bfloat16 [128, 64, 64], P('grid'), may hold values from 0.099609375 to 1.8984375
Outputs:
- subgrids: float32 [64, 1024, 128], P('band', 'grid')
The draws below stay inside these ranges and needn't reach their ends.
Inputs may be any that keep to these rules, and one draw needn't show every extreme that they name: `block_subgrid`: global subgrid numbers; subgrid g is owned by grid index g // 8. In each band the 128 blocks of one grid index name one owner at most 2 times, and one owner, drawn from the seed, exactly 2 times from every grid index. `block_stations`: the two stations of a block differ.
All inputs are finite; a program needn't handle non-finite values.
Results may differ from the reference program's by a relative error of at most 0.0046.
Values may be sent and summed in bfloat16 or wider, within the bound.
No kernel may reach another device: no remote copies, remote signals or barrier semaphores. Data moves between devices by JAX's collectives and lax.ppermute only.
A program may use at most 64 MiB of HBM per device.

```python
import math
import jax
import jax.numpy as jnp
from jax import lax

SUB = 64
TS = 16
CH = 24
NB = 128
SG_DEV = 8
CAP = 2
NBLK = 16384
NSUBG = 1024
STATIONS = 128
N_GRID = 128
N_BAND = 4


def draw_block_subgrid(key, part):
    key = jax.random.fold_in(key, 11)
    position_sum = N_GRID * CAP

    def one_band(band_random_key):
        popular_key, reward_key, jitter_key, nearby_key, ordering_key = jax.random.split(band_random_key, 5)
        hot_owner = jax.random.randint(popular_key, (), 0, N_GRID)
        holder_reward = jax.random.randint(reward_key, (N_GRID,), 0, 4) * 1024
        position_holder = jnp.arange(position_sum, dtype=jnp.int32) // CAP
        position_labels = jnp.arange(position_sum, dtype=jnp.int32)
        rating_jitter = jax.random.randint(jitter_key, (N_GRID, position_sum), 0, 4096)
        position_rating = (rating_jitter + holder_reward[position_holder][None, :]) * position_sum + position_labels[None, :]
        forced = (1 << 28) + position_labels
        position_rating = jnp.where((position_holder == hot_owner)[None, :], forced[None, :], position_rating)
        chosen = lax.top_k(position_rating, NB)[1]
        owner_of = chosen // CAP
        local_index = jax.random.randint(nearby_key, (N_GRID, NB), 0, SG_DEV)
        numbers = owner_of * SG_DEV + local_index
        row_keys = jax.random.split(ordering_key, N_GRID)
        shuffled = jax.vmap(jax.random.permutation)(row_keys, numbers)
        return shuffled.reshape(NBLK).astype(jnp.int32)
    band_keys = jax.random.split(key, N_BAND)
    return jax.vmap(one_band)(band_keys)


def draw_block_stations(key, part):
    key = jax.random.fold_in(key, 23)
    key_one, key_two = jax.random.split(key)
    station_one = jax.random.randint(key_one, (NBLK,), 0, STATIONS)
    offset = jax.random.randint(key_two, (NBLK,), 1, STATIONS)
    station_two = (station_one + offset) % STATIONS
    return jnp.stack([station_one, station_two], axis=1).astype(jnp.int32)


def levels(key, dims, pieces, least, largest):
    factor_of = 1.0
    for dim, parts in pieces:
        heights = jax.random.uniform(jax.random.fold_in(jax.random.fold_in(key, 6), dim), (parts,), jnp.float32, least / len(pieces), largest / len(pieces))
        factor_of = factor_of * jnp.repeat(jnp.exp(heights), dims[dim] // parts).reshape((-1,) + (1,) * (len(dims) - 1 - dim))
    return factor_of


def bell_draw(stream_key, dims, deviation, bound, cuts=(), kind=jnp.bfloat16):
    drawn = deviation * jax.random.normal(stream_key, dims, jnp.float32)
    if cuts:
        drawn = drawn * levels(stream_key, dims, cuts, -0.22, 0.18)
    return jnp.clip(drawn, -bound, bound).astype(kind)


def setup_inputs(seed: int = 0) -> dict:
    splits = jax.random.split(jax.random.key(seed), 8)
    visibility = bell_draw(splits[0], (N_BAND, NBLK, 2, TS * CH), 1.0, 6.0, ((0, 4), (1, 128)), jnp.float32)
    weights = jnp.clip(jnp.exp(math.log(2.0) - 2.3025851 * jax.random.uniform(splits[1], (N_BAND, NBLK, TS * CH), jnp.float32) ** levels(splits[1], (N_BAND, NBLK, TS * CH), ((0, 4), (1, 128)), -0.2, 0.2)), 0.2, 2.0)
    block_uv = jnp.clip(jax.random.uniform(splits[2], (NBLK, 2, TS), jnp.float32, -19.0, 19.0) * levels(splits[2], (NBLK, 2, TS), ((0, 128),), -0.4, 0.0), -19.0, 19.0)
    chan_ratio = jnp.clip(jnp.exp(math.log(1.0) - 0.5108256 * jax.random.uniform(splits[3], (N_BAND, CH), jnp.float32) ** levels(splits[3], (N_BAND, CH), ((0, 4),), -0.2, 0.2)), 0.6, 1.0)
    block_subgrid = draw_block_subgrid(jax.random.fold_in(splits[7], 71), 0)
    block_stations = draw_block_stations(jax.random.fold_in(splits[7], 71), 0)
    screens = jnp.clip(1.0 + 0.18 * jax.random.normal(splits[6], (STATIONS, SUB, SUB), jnp.float32), 0.099609375, 1.8984375).astype(jnp.bfloat16)
    return {"visibility": visibility, "weights": weights, "block_uv": block_uv, "chan_ratio": chan_ratio, "block_subgrid": block_subgrid, "block_stations": block_stations, "screens": screens}


def phase_angles(coords, chan_scale, grid_side):
    blocks = coords.shape[0]
    vis_len = coords.shape[2] * chan_scale.shape[0]
    u_coord = (coords[:, 0, :, None] * chan_scale[None, None, :]).reshape(blocks, vis_len)
    v_coord = (coords[:, 1, :, None] * chan_scale[None, None, :]).reshape(blocks, vis_len)
    centred = jnp.arange(grid_side).astype(jnp.float32) - grid_side / 2
    factor = 2.0 * math.pi / grid_side
    across_phase = factor * u_coord[:, None, :] * centred[None, :, None]
    down_phase = factor * v_coord[:, :, None] * centred[None, None, :]
    return (across_phase, down_phase)

def image_blocks(weighted, coords, chan_scale, station_one, station_two, screen_table):
    grid_side = screen_table.shape[1]
    vis_len = weighted.shape[2]
    across_phase, down_phase = phase_angles(coords, chan_scale, grid_side)
    cos_across = jnp.cos(across_phase)
    sin_across = jnp.sin(across_phase)
    real_vis = weighted[:, 0, None, :]
    imag_vis = weighted[:, 1, None, :]
    left_rows = jnp.concatenate([real_vis * cos_across - imag_vis * sin_across, real_vis * sin_across + imag_vis * cos_across], axis=1).astype(jnp.bfloat16)
    right_cols = jnp.concatenate([jnp.cos(down_phase), jnp.sin(down_phase)], axis=2).astype(jnp.bfloat16)
    products = jnp.einsum('gxk,gky->gxy', left_rows.astype(jnp.float32), right_cols.astype(jnp.float32))
    real_img = (products[:, :grid_side, :grid_side] - products[:, grid_side:, grid_side:]) / vis_len
    imag_img = (products[:, :grid_side, grid_side:] + products[:, grid_side:, :grid_side]) / vis_len
    beam_gain = screen_table[station_one].astype(jnp.float32) * screen_table[station_two].astype(jnp.float32)
    return jnp.concatenate([beam_gain * real_img, beam_gain * imag_img], axis=2).astype(jnp.bfloat16)

def dft_parts(row_index, col_index, grid_side):
    phase = (row_index[:, None] * col_index[None, :] % grid_side).astype(jnp.float32) * (2.0 * math.pi / grid_side)
    norm = 1.0 / math.sqrt(grid_side)
    return (jnp.cos(phase) * norm, -jnp.sin(phase) * norm)

def column_pass(image_stack):
    grid_side = image_stack.shape[1]
    pixel_index = jnp.arange(grid_side, dtype=jnp.int32)
    taper_line = jnp.sin(math.pi * (pixel_index.astype(jnp.float32) + 0.5) / grid_side)
    complete_window = taper_line[:, None] * jnp.concatenate([taper_line, taper_line])[None, :]
    cos_part, sin_part = dft_parts(pixel_index, pixel_index, grid_side)
    column_matrix = jnp.concatenate([jnp.concatenate([cos_part, sin_part], axis=1), jnp.concatenate([-sin_part, cos_part], axis=1)], axis=0)
    column_list = jnp.einsum('ste,ep->stp', image_stack * complete_window[None], column_matrix, precision=lax.Precision.HIGHEST)
    exchanged_rows = jnp.concatenate([-column_list[:, :, grid_side:], column_list[:, :, :grid_side]], axis=2)
    return (column_list, exchanged_rows)

def row_pass(column_list, exchanged_rows, row_index):
    grid_side = column_list.shape[1]
    pixel_index = jnp.arange(grid_side, dtype=jnp.int32)
    cosine_rows, sine_rows = dft_parts(row_index, pixel_index, grid_side)
    leading_term = jnp.einsum('ar,prw->apw', cosine_rows, column_list, precision=lax.Precision.HIGHEST)
    return leading_term + jnp.einsum('ar,prw->apw', sine_rows, exchanged_rows, precision=lax.Precision.HIGHEST)

def rows_from(source_array, first_row, row_total):
    return lax.dynamic_slice_in_dim(source_array, first_row, row_total, 0)

def reference(visibility, weights, block_uv, chan_ratio, block_subgrid, block_stations, screens):
    running = jnp.zeros((SUB, NSUBG, 2 * SUB), jnp.float32)
    for band_index in range(N_BAND):
        chan_scale = chan_ratio[band_index]
        band_vis = visibility[band_index]
        band_weights = weights[band_index]
        band_targets = block_subgrid[band_index]

        def scan_step(accumulated, group_index):
            first_row = (group_index * NB).astype(jnp.int32)
            weighted = rows_from(band_vis, first_row, NB) * rows_from(band_weights, first_row, NB)[:, None, :]
            stations = rows_from(block_stations, first_row, NB)
            image_stack = image_blocks(weighted, rows_from(block_uv, first_row, NB), chan_scale, stations[:, 0], stations[:, 1], screens)
            targets = rows_from(band_targets, first_row, NB)
            accumulated = accumulated.at[targets].add(image_stack.astype(jnp.float32).reshape(NB, SUB * 2 * SUB))
            return (accumulated, None)
        accumulated = lax.scan(scan_step, jnp.zeros((NSUBG, SUB * 2 * SUB), jnp.float32), jnp.arange(N_GRID, dtype=jnp.int32))[0]
        column_list, exchanged_rows = column_pass(accumulated.reshape(NSUBG, SUB, 2 * SUB))
        running = running + row_pass(column_list, exchanged_rows, jnp.arange(SUB, dtype=jnp.int32))
    return running
```

```python
import math

import jax
import jax.numpy as jnp
import numpy as np
from jax import lax
from jax.experimental import pallas as pl
from jax.experimental.pallas import tpu as pltpu
from jax.sharding import PartitionSpec as P

SUB = 64
TS = 16
CH = 24
VIS = TS * CH
SG_DEV = 8
CAP = 2
LANES = 128
CHUNKS = VIS // LANES
SLOT_ROWS = 8
HALF_ROWS = SUB * SUB // 2 // LANES
MSG_ROWS = CAP * SLOT_ROWS + HALF_ROWS

ACROSS = np.array([a + s * (b + 0.5) for a in (-24, -8, 8, 24) for s in (1, -1) for b in range(8)])
DOWN_HALF = np.array([a + s * (b + 0.5) for a in (8, 24) for s in (1, -1) for b in range(8)])
DOWN = np.concatenate([DOWN_HALF, -DOWN_HALF])
PERM_X = (ACROSS + 31.5).astype(np.int64)
PERM_Y = (DOWN + 31.5).astype(np.int64)


def taper_and_dft():
    taper = np.sin(math.pi * (np.arange(SUB) + 0.5) / SUB)
    window = taper[PERM_Y][:, None] * taper[PERM_X][None, :] / VIS
    window = np.concatenate([window, window], axis=1)
    dft = np.exp(-2j * math.pi * np.outer(np.arange(SUB), np.arange(SUB)) / SUB) / math.sqrt(SUB)

    def real_form(perm):
        part = dft[:, perm].T
        return np.block([[part.real, part.imag], [-part.imag, part.real]])

    return (
        window.astype(np.float32),
        real_form(PERM_X).astype(np.float32),
        real_form(PERM_Y).astype(np.float32),
    )


def coordinate_spread():
    spread = np.zeros((LANES, 2 * VIS), np.float32)
    for axis in range(2):
        for piece in range(3):
            for t in range(TS):
                spread[(axis * 3 + piece) * TS + t, axis * VIS + t * CH : axis * VIS + (t + 1) * CH] = 1.0
    return spread


def sincos(angle):
    square = angle * angle
    sine = angle * (
        1.0
        + square
        * (
            -1.0 / 6
            + square * (1.0 / 120 + square * (-1.0 / 5040 + square * (1.0 / 362880)))
        )
    )
    cosine = 1.0 + square * (
        -0.5
        + square
        * (1.0 / 24 + square * (-1.0 / 720 + square * (1.0 / 40320 + square * (-1.0 / 3628800))))
    )
    return cosine, sine


def doubled(cosine, sine):
    twice = cosine + cosine
    return twice * cosine - 1.0, twice * sine


def half_steps(cosine, sine, cos_full):
    twice = cos_full + cos_full
    cos_list = [cosine, cosine * (twice - 1.0)]
    sin_list = [sine, sine * (twice + 1.0)]
    for _ in range(6):
        cos_list.append(twice * cos_list[-1] - cos_list[-2])
        sin_list.append(twice * sin_list[-1] - sin_list[-2])
    return cos_list, sin_list


def grid_kernel(
    tags,
    recv,
    other,
    scale,
    spread,
    window,
    across_dft,
    down_dft,
    out,
    rows,
    angles,
    beams,
    anchors,
    steps,
    total,
):
    sources = recv.shape[0]
    core = lax.rem(lax.axis_index("grid"), 2)
    lane = lax.broadcasted_iota(jnp.int32, (8, LANES), 1)
    low = lane < SUB

    def unpack(i, carry):
        rows[pl.ds(pl.multiple_of(i * 16, 16), 16), :] = recv[i, 0:16, :].astype(jnp.float32)
        mine = recv[i, 16:32, :].astype(jnp.float32)
        theirs = other[i].astype(jnp.float32)
        for half in range(2):
            part = jnp.where(core == half, mine, theirs)
            turned = pltpu.roll(part, SUB, 1)
            for j in range(2):
                a = part[8 * j : 8 * j + 8]
                b = turned[8 * j : 8 * j + 8]
                beams[i, half * 32 + j * 8 : half * 32 + j * 8 + 8, :] = jnp.where(low, a, b)
                beams[i, half * 32 + 16 + j * 8 : half * 32 + 16 + j * 8 + 8, :] = jnp.where(low, b, a)
        return carry

    lax.fori_loop(0, sources, unpack, 0, unroll=4)
    slots = sources * CAP
    coords = rows[pl.ds(6, slots, stride=SLOT_ROWS), :].astype(jnp.bfloat16)
    angles[...] = jnp.dot(coords, spread[...], preferred_element_type=jnp.float32) * scale[...]
    total[...] = jnp.zeros_like(total)
    sign = jnp.where(lax.broadcasted_iota(jnp.int32, (32, LANES), 1) < SUB, -1.0, 1.0)

    def anchor_row(part, chunk):
        return part * CHUNKS + chunk

    def group(g, carry):
        for c in range(CHUNKS):
            real = rows[pl.ds(g * 64 + c, 8, stride=SLOT_ROWS), :]
            imag = rows[pl.ds(g * 64 + CHUNKS + c, 8, stride=SLOT_ROWS), :]
            at = pl.ds(pl.multiple_of(g * 8, 8), 8)
            cu, su = sincos(angles[at, c * LANES : (c + 1) * LANES])
            cv, sv = sincos(angles[at, VIS + c * LANES : VIS + (c + 1) * LANES])
            cc = cu * cv - su * sv
            ss = su * cv + cu * sv
            xr = real * cc + imag * ss
            xi = imag * cc - real * ss
            for axis, (cosine, sine) in enumerate(((cu, su), (cv, sv))):
                c1, s1 = doubled(cosine, sine)
                cos_list, sin_list = half_steps(cosine, sine, c1)
                for b in range(8):
                    for part, value in ((2 * axis, cos_list[b]), (2 * axis + 1, sin_list[b])):
                        steps[pl.ds((part * CHUNKS + c) * 8 + b, 8, stride=4 * CHUNKS * 8), :] = value
                c8, s8 = doubled(*doubled(*doubled(c1, s1)))
                c16, s16 = doubled(c8, s8)
                twice = c8 + c8
                c24, s24 = twice * c16 - c8, twice * s16 - s8
                if axis == 0:
                    values = []
                    for ca, sa in ((c24, s24), (c8, s8)):
                        p, q, r, t = xr * ca, xi * sa, xr * sa, xi * ca
                        values.append(((p + q, t - r), (p - q, t + r)))
                    ordered = (values[0][0], values[1][0], values[1][1], values[0][1])
                    for a in range(4):
                        for k in range(2):
                            anchors[anchor_row(2 * a + k, c)] = ordered[a][k]
                else:
                    for a, pair in enumerate(((c8, s8), (c24, s24))):
                        for k in range(2):
                            anchors[anchor_row(8 + 2 * a + k, c)] = pair[k]
        for s in range(8):

            def step(part, c):
                first = ((s * 4 + part) * CHUNKS + c) * 8
                return steps[first : first + 8, :]

            def anchor(part, c):
                return jnp.broadcast_to(anchors[anchor_row(part, c), s : s + 1, :], (8, LANES))

            left = [[None] * CHUNKS for _ in range(8)]
            right = [[None] * CHUNKS for _ in range(4)]
            for c in range(CHUNKS):
                d, e = step(0, c), step(1, c)
                for a in range(4):
                    pr, pi = anchor(2 * a, c), anchor(2 * a + 1, c)
                    rd, ie, re, id_ = pr * d, pi * e, pr * e, pi * d
                    left[a][c] = jnp.concatenate([rd - ie, rd + ie], axis=0).astype(jnp.bfloat16)
                    left[4 + a][c] = jnp.concatenate([id_ + re, id_ - re], axis=0).astype(jnp.bfloat16)
                d, e = step(2, c), step(3, c)
                for a in range(2):
                    ca, sa = anchor(8 + 2 * a, c), anchor(9 + 2 * a, c)
                    cd, se, sd, ce = ca * d, sa * e, sa * d, ca * e
                    right[a][c] = jnp.concatenate([cd - se, cd + se], axis=0).astype(jnp.bfloat16)
                    right[2 + a][c] = jnp.concatenate([sd + ce, sd - ce], axis=0).astype(jnp.bfloat16)
            left_all = jnp.concatenate([jnp.concatenate(r, axis=1) for r in left], axis=0)
            right_all = jnp.concatenate([jnp.concatenate(r, axis=1) for r in right], axis=0)
            product = lax.dot_general(
                right_all, left_all, (((1,), (1,)), ((), ())), preferred_element_type=jnp.float32
            )
            top = product[:32]
            turned = pltpu.roll(product[32:], SUB, 1) * sign
            image = jnp.concatenate([top + turned, top - turned], axis=0)
            slot = g * 8 + s
            target = tags[3 * slot]
            gain = beams[tags[3 * slot + 1]] * beams[tags[3 * slot + 2]]
            total[target] += gain * image
        return carry

    lax.fori_loop(0, slots // 8, group, 0)
    exact = lax.Precision.HIGHEST
    for g in range(SG_DEV):
        tapered = total[g] * window[...]
        first = jnp.dot(tapered, across_dft[...], precision=exact, preferred_element_type=jnp.float32)
        stacked = jnp.concatenate([first[:, :SUB], first[:, SUB:]], axis=0)
        second = lax.dot_general(
            stacked,
            down_dft[...],
            (((0,), (0,)), ((), ())),
            precision=exact,
            preferred_element_type=jnp.float32,
        )
        bands = out.shape[0]
        each = SUB // bands
        for b in range(bands):
            out[b, g] = second[b * each : (b + 1) * each]


def packed_blocks(visibility, weights, block_uv, targets, stations, grid_count):
    blocks = visibility.shape[0]
    owner = targets // SG_DEV
    order = jnp.arange(blocks, dtype=jnp.int32)
    earlier = (owner[:, None] == owner[None, :]) & (order[:, None] < order[None, :])
    rank = jnp.sum(earlier.astype(jnp.int32), axis=0)
    position = owner * CAP + rank
    choose = (jnp.arange(grid_count * CAP, dtype=jnp.int32)[:, None] == position[None, :]).astype(
        jnp.bfloat16
    )
    weighted = (visibility * weights[:, None, :]).reshape(blocks, 2 * VIS).astype(jnp.bfloat16)
    high = lax.reduce_precision(block_uv, 8, 7)
    rest = block_uv - high
    middle = lax.reduce_precision(rest, 8, 7)
    pieces = jnp.stack([high, middle, rest - middle], axis=2).reshape(blocks, 2 * 3 * TS)
    numbers = jnp.concatenate([(targets % SG_DEV)[:, None], stations], axis=1).astype(jnp.float32)
    line = jnp.concatenate([pieces, numbers], axis=1).astype(jnp.bfloat16)
    line = jnp.concatenate(
        [weighted, line, jnp.zeros((blocks, SLOT_ROWS * LANES - 2 * VIS - line.shape[1]), jnp.bfloat16)],
        axis=1,
    )
    placed = jnp.dot(choose, line, preferred_element_type=jnp.float32).astype(jnp.bfloat16)
    return placed.reshape(grid_count, CAP * SLOT_ROWS, LANES)


def screen_halves(screen):
    turn_y = np.zeros((SUB, SUB), np.float32)
    turn_y[np.arange(SUB), PERM_Y] = 1.0
    turn_x = np.zeros((SUB, SUB), np.float32)
    turn_x[np.arange(SUB), PERM_X] = 1.0
    turned = jnp.dot(turn_y.astype(jnp.bfloat16), screen.T, preferred_element_type=jnp.float32)
    turned = jnp.dot(
        turned.astype(jnp.bfloat16), turn_x.T.astype(jnp.bfloat16), preferred_element_type=jnp.float32
    ).astype(jnp.bfloat16)
    halves = turned.reshape(2, 2, HALF_ROWS, SUB)
    return jnp.concatenate([halves[:, 0], halves[:, 1]], axis=2)


def gridded(tags, recv, other, scale, bands):
    slots = recv.shape[0] * CAP
    window, across_dft, down_dft = taper_and_dft()
    vmem = pl.BlockSpec(memory_space=pltpu.VMEM)
    return pl.pallas_call(
        grid_kernel,
        out_shape=jax.ShapeDtypeStruct((bands, SG_DEV, SUB // bands, LANES), jnp.float32),
        in_specs=[pl.BlockSpec(memory_space=pltpu.SMEM)] + [vmem] * 7,
        out_specs=vmem,
        scratch_shapes=[
            pltpu.VMEM((slots * SLOT_ROWS, LANES), jnp.float32),
            pltpu.VMEM((slots, 2 * VIS), jnp.float32),
            pltpu.VMEM((recv.shape[0], SUB, LANES), jnp.float32),
            pltpu.VMEM((12 * CHUNKS, 8, LANES), jnp.float32),
            pltpu.VMEM((8 * 4 * CHUNKS * 8, LANES), jnp.float32),
            pltpu.VMEM((SG_DEV, SUB, LANES), jnp.float32),
        ],
        compiler_params=pltpu.CompilerParams(vmem_limit_bytes=40 * 1024 * 1024),
        name="grid_blocks",
    )(
        tags,
        recv,
        other,
        scale,
        jnp.asarray(coordinate_spread(), jnp.bfloat16),
        jnp.asarray(window),
        jnp.asarray(across_dft),
        jnp.asarray(down_dft),
    )


def shards(visibility, weights, block_uv, chan_ratio, block_subgrid, block_stations, screens):
    grid_count = lax.axis_size("grid")
    bands = lax.axis_size("band")
    placed = packed_blocks(
        visibility[0], weights[0], block_uv, block_subgrid[0], block_stations, grid_count
    )
    halves = screen_halves(screens[0])
    sent_halves = jnp.broadcast_to(halves[None], (grid_count // 2,) + halves.shape).reshape(
        grid_count, HALF_ROWS, LANES
    )
    message = jnp.concatenate([placed, sent_halves], axis=1)
    recv = lax.all_to_all(message, "grid", split_axis=0, concat_axis=0, tiled=True)
    other = lax.ppermute(
        recv[:, CAP * SLOT_ROWS :], "grid", [(i, i ^ 1) for i in range(grid_count)]
    )
    first = 2 * 3 * TS
    tags = recv[:, : CAP * SLOT_ROWS].reshape(grid_count * CAP, SLOT_ROWS, LANES)[
        :, 2 * CHUNKS, first : first + 3
    ]
    tags = tags.astype(jnp.int32).reshape(-1)
    scale = jnp.tile(chan_ratio[0] * (math.pi / SUB), 2 * TS)[None, :]
    rows = gridded(tags, recv, other, scale, bands)
    parts = lax.all_to_all(rows, "band", split_axis=0, concat_axis=0, tiled=True)
    return jnp.transpose(jnp.sum(parts, axis=0), (1, 0, 2))


def solution(mesh):
    in_specs = (
        P("band", "grid", None, None),
        P("band", "grid", None),
        P("grid", None, None),
        P("band", None),
        P("band", "grid"),
        P("grid", None),
        P("grid", None, None),
    )
    out_specs = P("band", "grid", None)
    return jax.shard_map(shards, mesh=mesh, in_specs=in_specs, out_specs=out_specs, check_vma=False)
```

```python
import math

import jax
import jax.numpy as jnp
import numpy as np
from jax import lax
from jax.experimental import pallas as pl
from jax.experimental.pallas import tpu as pltpu
from jax.sharding import PartitionSpec as P

SUB = 64
TS = 16
CH = 24
VIS = TS * CH
SG_DEV = 8
CAP = 2
LANES = 128
CHUNKS = VIS // LANES
GROUPS_A_TURN = 8
SLOT_ROWS = 8
HALF_ROWS = SUB * SUB // 2 // LANES
MSG_ROWS = CAP * SLOT_ROWS + HALF_ROWS
PITCH = 264

ACROSS = np.array([a + s * (b + 0.5) for a in (-24, -8, 8, 24) for s in (1, -1) for b in range(8)])
DOWN_HALF = np.array([a + s * (b + 0.5) for a in (8, 24) for s in (1, -1) for b in range(8)])
DOWN = np.concatenate([DOWN_HALF, -DOWN_HALF])
PERM_X = (ACROSS + 31.5).astype(np.int64)
PERM_Y = (DOWN + 31.5).astype(np.int64)


def taper_and_dft():
    taper = np.sin(math.pi * (np.arange(SUB) + 0.5) / SUB)
    window = taper[PERM_Y][:, None] * taper[PERM_X][None, :] / VIS
    window = np.concatenate([window, window], axis=1)
    dft = np.exp(-2j * math.pi * np.outer(np.arange(SUB), np.arange(SUB)) / SUB) / math.sqrt(SUB)

    def real_form(perm):
        part = dft[:, perm].T
        return np.block([[part.real, part.imag], [-part.imag, part.real]])

    return (
        window.astype(np.float32),
        real_form(PERM_X).astype(np.float32),
        real_form(PERM_Y).astype(np.float32),
    )


def coordinate_spread():
    spread = np.zeros((LANES, 2 * VIS), np.float32)
    for axis in range(2):
        for piece in range(3):
            for t in range(TS):
                spread[(piece * 2 + axis) * TS + t, axis * VIS + t * CH : axis * VIS + (t + 1) * CH] = 1.0
    return spread


def sincos(angle):
    square = angle * angle
    sine = angle * (
        1.0
        + square
        * (
            -1.0 / 6
            + square * (1.0 / 120 + square * (-1.0 / 5040 + square * (1.0 / 362880)))
        )
    )
    cosine = 1.0 + square * (
        -0.5
        + square
        * (1.0 / 24 + square * (-1.0 / 720 + square * (1.0 / 40320 + square * (-1.0 / 3628800))))
    )
    return cosine, sine


def doubled(cosine, sine):
    twice = cosine + cosine
    return twice * cosine - 1.0, twice * sine


def half_steps(cosine, sine, cos_full):
    twice = cos_full + cos_full
    cos_list = [cosine, cosine * (twice - 1.0)]
    sin_list = [sine, sine * (twice + 1.0)]
    for _ in range(6):
        cos_list.append(twice * cos_list[-1] - cos_list[-2])
        sin_list.append(twice * sin_list[-1] - sin_list[-2])
    return cos_list, sin_list


def grid_kernel(
    tags,
    recv,
    other,
    scale,
    spread,
    window,
    across_dft,
    down_dft,
    out,
    rows,
    angles,
    beams,
    total,
    *buffers,
):
    sources = recv.shape[0]
    core = lax.rem(lax.axis_index("grid"), 2)
    lane = lax.broadcasted_iota(jnp.int32, (8, LANES), 1)
    low = lane < SUB

    def unpack(i, carry):
        rows[pl.ds(pl.multiple_of(i * 16, 16), 16), :] = recv[i, 0:16, :].astype(jnp.float32)
        mine = recv[i, 16:32, :].astype(jnp.float32)
        theirs = other[i].astype(jnp.float32)
        for half in range(2):
            part = jnp.where(core == half, mine, theirs)
            turned = pltpu.roll(part, SUB, 1)
            for j in range(2):
                a = part[8 * j : 8 * j + 8]
                b = turned[8 * j : 8 * j + 8]
                beams[i, half * 32 + j * 8 : half * 32 + j * 8 + 8, :] = jnp.where(low, a, b)
                beams[i, half * 32 + 16 + j * 8 : half * 32 + 16 + j * 8 + 8, :] = jnp.where(low, b, a)
        return carry

    lax.fori_loop(0, sources, unpack, 0, unroll=16)
    slots = sources * CAP
    coords = rows[pl.ds(6, slots, stride=SLOT_ROWS), :].astype(jnp.bfloat16)
    angles[...] = jnp.dot(coords, spread[...], preferred_element_type=jnp.float32) * scale[...]
    total[...] = jnp.zeros_like(total)
    sign = jnp.where(lax.broadcasted_iota(jnp.int32, (32, LANES), 1) < SUB, -1.0, 1.0)

    def anchor_row(part, chunk):
        return part * CHUNKS + chunk

    def base(g, anchors, steps):
        for c in range(CHUNKS):
            real = rows[pl.ds(g * 64 + c, 8, stride=SLOT_ROWS), :]
            imag = rows[pl.ds(g * 64 + CHUNKS + c, 8, stride=SLOT_ROWS), :]
            at = pl.ds(pl.multiple_of(g * 8, 8), 8)
            cu, su = sincos(angles[at, c * LANES : (c + 1) * LANES])
            cv, sv = sincos(angles[at, VIS + c * LANES : VIS + (c + 1) * LANES])
            cc = cu * cv - su * sv
            ss = su * cv + cu * sv
            xr = real * cc + imag * ss
            xi = imag * cc - real * ss
            for axis, (cosine, sine) in enumerate(((cu, su), (cv, sv))):
                c1, s1 = doubled(cosine, sine)
                cos_list, sin_list = half_steps(cosine, sine, c1)
                for b in range(8):
                    for part, value in ((2 * axis, cos_list[b]), (2 * axis + 1, sin_list[b])):
                        first = (part * CHUNKS + c) * 64 + b * 8
                        steps[first : first + 8, :] = value
                c8, s8 = doubled(*doubled(*doubled(c1, s1)))
                c16, s16 = doubled(c8, s8)
                twice = c8 + c8
                c24, s24 = twice * c16 - c8, twice * s16 - s8
                if axis == 0:
                    values = []
                    for ca, sa in ((c24, s24), (c8, s8)):
                        p, q, r, t = xr * ca, xi * sa, xr * sa, xi * ca
                        values.append(((p + q, t - r), (p - q, t + r)))
                    ordered = (values[0][0], values[1][0], values[1][1], values[0][1])
                    for a in range(4):
                        for k in range(2):
                            anchors[anchor_row(2 * a + k, c)] = ordered[a][k]
                else:
                    for a, pair in enumerate(((c8, s8), (c24, s24))):
                        for k in range(2):
                            anchors[anchor_row(8 + 2 * a + k, c)] = pair[k]

    def expand(g, anchors, steps):
        for s in range(8):

            def step(part, c):
                return steps[pl.ds((part * CHUNKS + c) * 64 + s, 8, stride=8), :]

            def anchor(part, c):
                return jnp.broadcast_to(anchors[anchor_row(part, c), s : s + 1, :], (8, LANES))

            left = [[None] * CHUNKS for _ in range(8)]
            right = [[None] * CHUNKS for _ in range(4)]
            for c in range(CHUNKS):
                d, e = step(0, c), step(1, c)
                for a in range(4):
                    pr, pi = anchor(2 * a, c), anchor(2 * a + 1, c)
                    rd, ie, re, id_ = pr * d, pi * e, pr * e, pi * d
                    left[a][c] = jnp.concatenate([rd - ie, rd + ie], axis=0).astype(jnp.bfloat16)
                    left[4 + a][c] = jnp.concatenate([id_ + re, id_ - re], axis=0).astype(jnp.bfloat16)
                d, e = step(2, c), step(3, c)
                for a in range(2):
                    ca, sa = anchor(8 + 2 * a, c), anchor(9 + 2 * a, c)
                    cd, se, sd, ce = ca * d, sa * e, sa * d, ca * e
                    right[a][c] = jnp.concatenate([cd, se], axis=0).astype(jnp.bfloat16)
                    right[2 + a][c] = jnp.concatenate([sd, ce], axis=0).astype(jnp.bfloat16)
            left_all = jnp.concatenate([jnp.concatenate(r, axis=1) for r in left], axis=0)
            right_all = jnp.concatenate([jnp.concatenate(r, axis=1) for r in right], axis=0)
            product = lax.dot_general(
                right_all, left_all, (((1,), (1,)), ((), ())), preferred_element_type=jnp.float32
            )
            q = [product[8 * j : 8 * j + 8] for j in range(8)]
            top = jnp.concatenate([q[0] - q[1], q[0] + q[1], q[2] - q[3], q[2] + q[3]], axis=0)
            bottom = jnp.concatenate([q[4] + q[5], q[4] - q[5], q[6] + q[7], q[6] - q[7]], axis=0)
            turned = pltpu.roll(bottom, SUB, 1) * sign
            image = jnp.concatenate([top + turned, top - turned], axis=0)
            slot = g * 8 + s
            target = tags[3 * slot]
            gain = beams[tags[3 * slot + 1]] * beams[tags[3 * slot + 2]]
            total[target] += gain * image

    turns = slots // 8 // GROUPS_A_TURN

    def turn(i, carry):
        for j in range(GROUPS_A_TURN):
            at = 2 * (j % 2)
            base(GROUPS_A_TURN * i + j, *buffers[at : at + 2])
            expand(GROUPS_A_TURN * i + j, *buffers[at : at + 2])
        return carry

    lax.fori_loop(0, turns, turn, 0)
    exact = lax.Precision.HIGHEST
    for g in range(SG_DEV):
        tapered = total[g] * window[...]
        first = jnp.dot(tapered, across_dft[...], precision=exact, preferred_element_type=jnp.float32)
        stacked = jnp.concatenate([first[:, :SUB], first[:, SUB:]], axis=0)
        second = lax.dot_general(
            stacked,
            down_dft[...],
            (((0,), (0,)), ((), ())),
            precision=exact,
            preferred_element_type=jnp.float32,
        )
        bands = out.shape[0]
        each = SUB // bands
        for b in range(bands):
            out[b, g] = second[b * each : (b + 1) * each]


def pack_kernel(visibility, weights, coords, owned, stations, screen, turn_y, turn_x, out, placed):
    blocks = weights.shape[0]
    dests = out.shape[0]
    lined = jnp.broadcast_to((owned[...] // SG_DEV).astype(jnp.float32), (blocks, blocks))
    first = lax.broadcasted_iota(jnp.int32, (blocks, blocks), 0)
    second = lax.broadcasted_iota(jnp.int32, (blocks, blocks), 1)
    earlier = jnp.where((lined.T == lined) & (first < second), 1.0, 0.0)
    rank = jnp.sum(earlier, axis=0, keepdims=True)
    dest = lax.broadcasted_iota(jnp.int32, (dests, blocks), 0).astype(jnp.float32)
    here = jnp.broadcast_to(lined[:1], (dests, blocks)) == dest
    ranks = jnp.broadcast_to(rank, (dests, blocks))
    choose = jnp.concatenate(
        [jnp.where(here & (ranks == k), 1.0, 0.0) for k in range(CAP)], axis=0
    ).astype(jnp.bfloat16)
    for c in range(CHUNKS):
        weight = weights[:, c * LANES : (c + 1) * LANES]
        for k in range(2):
            weighted = visibility[:, k, c * LANES : (c + 1) * LANES] * weight
            at = (k * CHUNKS + c) * PITCH
            placed[at : at + CAP * dests, :] = jnp.dot(
                choose, weighted.astype(jnp.bfloat16), preferred_element_type=jnp.float32
            )
    rest = coords[...]
    pieces = []
    for _ in range(3):
        pieces.append(rest.astype(jnp.bfloat16).astype(jnp.float32))
        rest = rest - pieces[-1]
    local = (owned[...] % SG_DEV).astype(jnp.float32)
    numbers = jnp.concatenate(
        [local, stations[...].astype(jnp.float32), jnp.zeros((5, blocks), jnp.float32)], axis=0
    )
    empty = jnp.zeros((LANES - 3 * coords.shape[0] - 8, blocks), jnp.float32)
    line = jnp.concatenate(pieces + [numbers, empty], axis=0).astype(jnp.bfloat16)
    at = 2 * CHUNKS * PITCH
    placed[at : at + CAP * dests, :] = lax.dot_general(
        choose, line, (((1,), (1,)), ((), ())), preferred_element_type=jnp.float32
    )
    at = (2 * CHUNKS + 1) * PITCH
    placed[at : at + CAP * dests, :] = jnp.zeros((CAP * dests, LANES), jnp.float32)
    turned = lax.dot_general(
        turn_y[...], screen[...], (((1,), (1,)), ((), ())), preferred_element_type=jnp.float32
    ).astype(jnp.bfloat16)
    halves = []
    for h in range(2):
        sides = [
            jnp.dot(
                turned[32 * h + 16 * k : 32 * h + 16 * k + 16],
                turn_x[k],
                preferred_element_type=jnp.float32,
            )
            for k in range(2)
        ]
        halves.append((sides[0] + sides[1]).astype(jnp.bfloat16))

    def write(i, carry):
        for h in range(2):
            d = 2 * i + h
            rows = [
                placed[pl.ds(k * dests + d, SLOT_ROWS, stride=PITCH), :] for k in range(CAP)
            ]
            out[d, 0 : CAP * SLOT_ROWS, :] = jnp.concatenate(rows, axis=0).astype(jnp.bfloat16)
            out[d, CAP * SLOT_ROWS :, :] = halves[h]
        return carry

    lax.fori_loop(0, dests // 2, write, 0, unroll=8)


def packed(visibility, weights, block_uv, targets, stations, screen, grid_count):
    blocks = visibility.shape[0]
    turn_y = np.zeros((SUB, SUB), np.float32)
    turn_y[np.arange(SUB), PERM_Y] = 1.0
    turn_x = np.zeros((2, SUB, LANES), np.float32)
    for k in range(2):
        turn_x[k, PERM_X, k * SUB + np.arange(SUB)] = 1.0
    vmem = pl.BlockSpec(memory_space=pltpu.VMEM)
    return pl.pallas_call(
        pack_kernel,
        out_shape=jax.ShapeDtypeStruct((grid_count, MSG_ROWS, LANES), jnp.bfloat16),
        in_specs=[vmem] * 8,
        out_specs=vmem,
        scratch_shapes=[pltpu.VMEM((SLOT_ROWS * PITCH, LANES), jnp.float32)],
        compiler_params=pltpu.CompilerParams(vmem_limit_bytes=40 * 1024 * 1024),
        name="pack_blocks",
    )(
        visibility,
        weights,
        block_uv.transpose(1, 2, 0).reshape(2 * TS, blocks),
        targets,
        stations.T,
        screen,
        jnp.asarray(turn_y, jnp.bfloat16),
        jnp.asarray(turn_x, jnp.bfloat16),
    )


def gridded(tags, recv, other, scale, bands):
    slots = recv.shape[0] * CAP
    window, across_dft, down_dft = taper_and_dft()
    vmem = pl.BlockSpec(memory_space=pltpu.VMEM)
    return pl.pallas_call(
        grid_kernel,
        out_shape=jax.ShapeDtypeStruct((bands, SG_DEV, SUB // bands, LANES), jnp.float32),
        in_specs=[pl.BlockSpec(memory_space=pltpu.SMEM)] + [vmem] * 7,
        out_specs=vmem,
        scratch_shapes=[
            pltpu.VMEM((slots * SLOT_ROWS, LANES), jnp.float32),
            pltpu.VMEM((slots, 2 * VIS), jnp.float32),
            pltpu.VMEM((recv.shape[0], SUB, LANES), jnp.float32),
            pltpu.VMEM((SG_DEV, SUB, LANES), jnp.float32),
            pltpu.VMEM((12 * CHUNKS, 8, LANES), jnp.float32),
            pltpu.VMEM((4 * CHUNKS * 64, LANES), jnp.float32),
            pltpu.VMEM((12 * CHUNKS, 8, LANES), jnp.float32),
            pltpu.VMEM((4 * CHUNKS * 64, LANES), jnp.float32),
        ],
        compiler_params=pltpu.CompilerParams(vmem_limit_bytes=40 * 1024 * 1024),
        name="grid_blocks",
    )(
        tags,
        recv,
        other,
        scale,
        jnp.asarray(coordinate_spread(), jnp.bfloat16),
        jnp.asarray(window),
        jnp.asarray(across_dft),
        jnp.asarray(down_dft),
    )


def shards(visibility, weights, block_uv, chan_ratio, block_subgrid, block_stations, screens):
    grid_count = lax.axis_size("grid")
    bands = lax.axis_size("band")
    message = packed(
        visibility[0], weights[0], block_uv, block_subgrid, block_stations, screens[0], grid_count
    )
    recv = lax.all_to_all(message, "grid", split_axis=0, concat_axis=0, tiled=True)
    other = lax.ppermute(
        recv[:, CAP * SLOT_ROWS :], "grid", [(i, i ^ 1) for i in range(grid_count)]
    )
    first = 2 * 3 * TS
    tags = recv[:, : CAP * SLOT_ROWS].reshape(grid_count * CAP, SLOT_ROWS, LANES)[
        :, 2 * CHUNKS, first : first + 3
    ]
    tags = tags.astype(jnp.int32).reshape(-1)
    scale = jnp.tile(chan_ratio[0] * (math.pi / SUB), 2 * TS)[None, :]
    rows = gridded(tags, recv, other, scale, bands)
    parts = lax.all_to_all(rows, "band", split_axis=0, concat_axis=0, tiled=True)
    return jnp.transpose(jnp.sum(parts, axis=0), (1, 0, 2))


def solution(mesh):
    in_specs = (
        P("band", "grid", None, None),
        P("band", "grid", None),
        P("grid", None, None),
        P("band", None),
        P("band", "grid"),
        P("grid", None),
        P("grid", None, None),
    )
    out_specs = P("band", "grid", None)
    return jax.shard_map(shards, mesh=mesh, in_specs=in_specs, out_specs=out_specs, check_vma=False)
```

```python
import math

import jax
import jax.numpy as jnp
import numpy as np
from jax import lax
from jax.experimental import pallas as pl
from jax.experimental.pallas import tpu as pltpu
from jax.sharding import PartitionSpec as P

SUB = 64
TS = 16
CH = 24
VIS = TS * CH
SG_DEV = 8
CAP = 2
LANES = 128
CHUNKS = VIS // LANES
GROUPS_A_TURN = 8
SLOT_ROWS = 8
HALF_ROWS = SUB * SUB // 2 // LANES
MSG_ROWS = CAP * SLOT_ROWS + HALF_ROWS
PITCH = 264

ACROSS = np.array([a + s * (b + 0.5) for a in (-24, -8, 8, 24) for s in (1, -1) for b in range(8)])
DOWN_HALF = np.array([a + s * (b + 0.5) for a in (8, 24) for s in (1, -1) for b in range(8)])
DOWN = np.concatenate([DOWN_HALF, -DOWN_HALF])
PERM_X = (ACROSS + 31.5).astype(np.int64)
PERM_Y = (DOWN + 31.5).astype(np.int64)


def taper_and_dft():
    taper = np.sin(math.pi * (np.arange(SUB) + 0.5) / SUB)
    window = taper[PERM_Y][:, None] * taper[PERM_X][None, :] / VIS
    window = np.concatenate([window, window], axis=1)
    dft = np.exp(-2j * math.pi * np.outer(np.arange(SUB), np.arange(SUB)) / SUB) / math.sqrt(SUB)

    def real_form(perm):
        part = dft[:, perm].T
        return np.block([[part.real, part.imag], [-part.imag, part.real]])

    return (
        window.astype(np.float32),
        real_form(PERM_X).astype(np.float32),
        real_form(PERM_Y).astype(np.float32),
    )


def coordinate_spread():
    spread = np.zeros((LANES, 2 * VIS), np.float32)
    for axis in range(2):
        for piece in range(3):
            for t in range(TS):
                spread[(piece * 2 + axis) * TS + t, axis * VIS + t * CH : axis * VIS + (t + 1) * CH] = 1.0
    return spread


def sincos(angle):
    square = angle * angle
    sine = angle * (
        1.0
        + square
        * (
            -1.0 / 6
            + square * (1.0 / 120 + square * (-1.0 / 5040 + square * (1.0 / 362880)))
        )
    )
    cosine = 1.0 + square * (
        -0.5
        + square
        * (1.0 / 24 + square * (-1.0 / 720 + square * (1.0 / 40320 + square * (-1.0 / 3628800))))
    )
    return cosine, sine


def doubled(cosine, sine):
    twice = cosine + cosine
    return twice * cosine - 1.0, twice * sine


def half_steps(cosine, sine, cos_full):
    twice = cos_full + cos_full
    cos_list = [cosine, cosine * (twice - 1.0)]
    sin_list = [sine, sine * (twice + 1.0)]
    for _ in range(6):
        cos_list.append(twice * cos_list[-1] - cos_list[-2])
        sin_list.append(twice * sin_list[-1] - sin_list[-2])
    return cos_list, sin_list


def grid_kernel(
    tags,
    recv,
    other,
    scale,
    spread,
    window,
    across_dft,
    down_dft,
    out,
    rows,
    angles,
    beams,
    total,
    *buffers,
):
    sources = recv.shape[0]
    core = lax.rem(lax.axis_index("grid"), 2)
    lane = lax.broadcasted_iota(jnp.int32, (8, LANES), 1)
    low = lane < SUB

    def unpack(i, carry):
        rows[pl.ds(pl.multiple_of(i * 16, 16), 16), :] = recv[i, 0:16, :].astype(jnp.float32)
        mine = recv[i, 16:32, :].astype(jnp.float32)
        theirs = other[i].astype(jnp.float32)
        for half in range(2):
            part = jnp.where(core == half, mine, theirs)
            turned = pltpu.roll(part, SUB, 1)
            for j in range(2):
                a = part[8 * j : 8 * j + 8]
                b = turned[8 * j : 8 * j + 8]
                beams[i, half * 32 + j * 8 : half * 32 + j * 8 + 8, :] = jnp.where(low, a, b)
                beams[i, half * 32 + 16 + j * 8 : half * 32 + 16 + j * 8 + 8, :] = jnp.where(low, b, a)
        return carry

    lax.fori_loop(0, sources, unpack, 0, unroll=16)
    slots = sources * CAP
    coords = rows[pl.ds(6, slots, stride=SLOT_ROWS), :].astype(jnp.bfloat16)
    angles[...] = jnp.dot(coords, spread[...], preferred_element_type=jnp.float32) * scale[...]
    total[...] = jnp.zeros_like(total)
    sign = jnp.where(lax.broadcasted_iota(jnp.int32, (32, LANES), 1) < SUB, -1.0, 1.0)

    def anchor_row(part, chunk):
        return part * CHUNKS + chunk

    def base(g, anchors, steps):
        for c in range(CHUNKS):
            real = rows[pl.ds(g * 64 + c, 8, stride=SLOT_ROWS), :]
            imag = rows[pl.ds(g * 64 + CHUNKS + c, 8, stride=SLOT_ROWS), :]
            at = pl.ds(pl.multiple_of(g * 8, 8), 8)
            cu, su = sincos(angles[at, c * LANES : (c + 1) * LANES])
            cv, sv = sincos(angles[at, VIS + c * LANES : VIS + (c + 1) * LANES])
            cc = cu * cv - su * sv
            ss = su * cv + cu * sv
            xr = real * cc + imag * ss
            xi = imag * cc - real * ss
            for axis, (cosine, sine) in enumerate(((cu, su), (cv, sv))):
                c1, s1 = doubled(cosine, sine)
                cos_list, sin_list = half_steps(cosine, sine, c1)
                for b in range(8):
                    for part, value in ((2 * axis, cos_list[b]), (2 * axis + 1, sin_list[b])):
                        first = (part * CHUNKS + c) * 64 + b * 8
                        steps[first : first + 8, :] = value
                c8, s8 = doubled(*doubled(*doubled(c1, s1)))
                c16, s16 = doubled(c8, s8)
                twice = c8 + c8
                c24, s24 = twice * c16 - c8, twice * s16 - s8
                if axis == 0:
                    values = []
                    for ca, sa in ((c24, s24), (c8, s8)):
                        p, q, r, t = xr * ca, xi * sa, xr * sa, xi * ca
                        values.append(((p + q, t - r), (p - q, t + r)))
                    ordered = (values[0][0], values[1][0], values[1][1], values[0][1])
                    for a in range(4):
                        for k in range(2):
                            anchors[anchor_row(2 * a + k, c)] = ordered[a][k]
                else:
                    for a, pair in enumerate(((c8, s8), (c24, s24))):
                        for k in range(2):
                            anchors[anchor_row(8 + 2 * a + k, c)] = pair[k]

    def expand(g, anchors, steps):
        for s in range(8):

            def step(part, c):
                return steps[pl.ds((part * CHUNKS + c) * 64 + s, 8, stride=8), :]

            def anchor(part, c):
                return jnp.broadcast_to(anchors[anchor_row(part, c), s : s + 1, :], (8, LANES))

            left = [[None] * CHUNKS for _ in range(8)]
            right = [[None] * CHUNKS for _ in range(4)]
            for c in range(CHUNKS):
                d, e = step(0, c), step(1, c)
                for a in range(4):
                    pr, pi = anchor(2 * a, c), anchor(2 * a + 1, c)
                    rd, ie, re, id_ = pr * d, pi * e, pr * e, pi * d
                    left[a][c] = jnp.concatenate([rd - ie, rd + ie], axis=0).astype(jnp.bfloat16)
                    left[4 + a][c] = jnp.concatenate([id_ + re, id_ - re], axis=0).astype(jnp.bfloat16)
                d, e = step(2, c), step(3, c)
                for a in range(2):
                    ca, sa = anchor(8 + 2 * a, c), anchor(9 + 2 * a, c)
                    cd, se, sd, ce = ca * d, sa * e, sa * d, ca * e
                    right[a][c] = jnp.concatenate([cd, se], axis=0).astype(jnp.bfloat16)
                    right[2 + a][c] = jnp.concatenate([sd, ce], axis=0).astype(jnp.bfloat16)
            left_all = jnp.concatenate([jnp.concatenate(r, axis=1) for r in left], axis=0)
            right_all = jnp.concatenate([jnp.concatenate(r, axis=1) for r in right], axis=0)
            product = lax.dot_general(
                right_all, left_all, (((1,), (1,)), ((), ())), preferred_element_type=jnp.float32
            )
            q = [product[8 * j : 8 * j + 8] for j in range(8)]
            top = jnp.concatenate([q[0] - q[1], q[0] + q[1], q[2] - q[3], q[2] + q[3]], axis=0)
            bottom = jnp.concatenate([q[4] + q[5], q[4] - q[5], q[6] + q[7], q[6] - q[7]], axis=0)
            turned = pltpu.roll(bottom, SUB, 1) * sign
            image = jnp.concatenate([top + turned, top - turned], axis=0)
            slot = g * 8 + s
            target = tags[3 * slot]
            gain = beams[tags[3 * slot + 1]] * beams[tags[3 * slot + 2]]
            total[target] += gain * image

    turns = slots // 8 // GROUPS_A_TURN

    def turn(i, carry):
        for j in range(GROUPS_A_TURN):
            at = 2 * (j % 2)
            base(GROUPS_A_TURN * i + j, *buffers[at : at + 2])
            expand(GROUPS_A_TURN * i + j, *buffers[at : at + 2])
        return carry

    lax.fori_loop(0, turns, turn, 0)
    exact = lax.Precision.HIGHEST
    tapered = (total[...] * window[...]).reshape(SG_DEV * SUB, LANES)
    first = jnp.dot(tapered, across_dft[...], precision=exact, preferred_element_type=jnp.float32)
    bands = out.shape[0]
    each = SUB // bands
    for g in range(SG_DEV):
        mine = first[g * SUB : (g + 1) * SUB]
        stacked = jnp.concatenate([mine[:, :SUB], mine[:, SUB:]], axis=0)
        second = lax.dot_general(
            stacked,
            down_dft[...],
            (((0,), (0,)), ((), ())),
            precision=exact,
            preferred_element_type=jnp.float32,
        )
        for b in range(bands):
            out[b, :, g, :] = second[b * each : (b + 1) * each]


def pack_kernel(*refs):
    sources, out, placed, held, done = refs[:8], refs[8], refs[9], refs[10:18], refs[18]
    copies = [pltpu.make_async_copy(sources[i], held[i], done.at[i]) for i in range(8)]
    for copy in copies:
        copy.start()
    visibility, weights, coords, owned, stations, screen, turn_y, turn_x = held
    for copy in copies[2:]:
        copy.wait()
    blocks = weights.shape[0]
    dests = out.shape[0]
    lined = jnp.broadcast_to((owned[...] // SG_DEV).astype(jnp.float32), (blocks, blocks))
    first = lax.broadcasted_iota(jnp.int32, (blocks, blocks), 0)
    second = lax.broadcasted_iota(jnp.int32, (blocks, blocks), 1)
    earlier = jnp.where((lined.T == lined) & (first < second), 1.0, 0.0)
    rank = jnp.sum(earlier, axis=0, keepdims=True)
    dest = lax.broadcasted_iota(jnp.int32, (dests, blocks), 0).astype(jnp.float32)
    here = jnp.broadcast_to(lined[:1], (dests, blocks)) == dest
    ranks = jnp.broadcast_to(rank, (dests, blocks))
    choose = jnp.concatenate(
        [jnp.where(here & (ranks == k), 1.0, 0.0) for k in range(CAP)], axis=0
    ).astype(jnp.bfloat16)
    rest = coords[...]
    pieces = []
    for _ in range(3):
        pieces.append(rest.astype(jnp.bfloat16).astype(jnp.float32))
        rest = rest - pieces[-1]
    local = (owned[...] % SG_DEV).astype(jnp.float32)
    numbers = jnp.concatenate(
        [local, stations[...].astype(jnp.float32), jnp.zeros((5, blocks), jnp.float32)], axis=0
    )
    empty = jnp.zeros((LANES - 3 * coords.shape[0] - 8, blocks), jnp.float32)
    line = jnp.concatenate(pieces + [numbers, empty], axis=0).astype(jnp.bfloat16)
    at = 2 * CHUNKS * PITCH
    placed[at : at + CAP * dests, :] = lax.dot_general(
        choose, line, (((1,), (1,)), ((), ())), preferred_element_type=jnp.float32
    )
    at = (2 * CHUNKS + 1) * PITCH
    placed[at : at + CAP * dests, :] = jnp.zeros((CAP * dests, LANES), jnp.float32)
    turned = lax.dot_general(
        turn_y[...], screen[...], (((1,), (1,)), ((), ())), preferred_element_type=jnp.float32
    ).astype(jnp.bfloat16)
    halves = []
    for h in range(2):
        sides = [
            jnp.dot(
                turned[32 * h + 16 * k : 32 * h + 16 * k + 16],
                turn_x[k],
                preferred_element_type=jnp.float32,
            )
            for k in range(2)
        ]
        halves.append((sides[0] + sides[1]).astype(jnp.bfloat16))

    copies[1].wait()
    copies[0].wait()
    for c in range(CHUNKS):
        weight = weights[:, c * LANES : (c + 1) * LANES]
        for k in range(2):
            weighted = visibility[:, k, c * LANES : (c + 1) * LANES] * weight
            at = (k * CHUNKS + c) * PITCH
            placed[at : at + CAP * dests, :] = jnp.dot(
                choose, weighted.astype(jnp.bfloat16), preferred_element_type=jnp.float32
            )
    def write(i, carry):
        for h in range(2):
            d = 2 * i + h
            rows = [
                placed[pl.ds(k * dests + d, SLOT_ROWS, stride=PITCH), :] for k in range(CAP)
            ]
            out[d, 0 : CAP * SLOT_ROWS, :] = jnp.concatenate(rows, axis=0).astype(jnp.bfloat16)
            out[d, CAP * SLOT_ROWS :, :] = halves[h]
        return carry

    lax.fori_loop(0, dests // 2, write, 0, unroll=8)


def packed(visibility, weights, block_uv, targets, stations, screen, grid_count):
    blocks = visibility.shape[0]
    turn_y = np.zeros((SUB, SUB), np.float32)
    turn_y[np.arange(SUB), PERM_Y] = 1.0
    turn_x = np.zeros((2, SUB, LANES), np.float32)
    for k in range(2):
        turn_x[k, PERM_X, k * SUB + np.arange(SUB)] = 1.0
    operands = [
        visibility,
        weights,
        block_uv.transpose(1, 2, 0).reshape(2 * TS, blocks),
        targets,
        stations.T,
        screen,
        jnp.asarray(turn_y, jnp.bfloat16),
        jnp.asarray(turn_x, jnp.bfloat16),
    ]
    return pl.pallas_call(
        pack_kernel,
        out_shape=jax.ShapeDtypeStruct((grid_count, MSG_ROWS, LANES), jnp.bfloat16),
        in_specs=[pl.BlockSpec(memory_space=pltpu.HBM)] * 8,
        out_specs=pl.BlockSpec(memory_space=pltpu.VMEM),
        scratch_shapes=[pltpu.VMEM((SLOT_ROWS * PITCH, LANES), jnp.float32)]
        + [pltpu.VMEM(x.shape, x.dtype) for x in operands]
        + [pltpu.SemaphoreType.DMA((8,))],
        compiler_params=pltpu.CompilerParams(vmem_limit_bytes=56 * 1024 * 1024),
        name="pack_blocks",
    )(*operands)


def gridded(tags, recv, other, scale, bands):
    slots = recv.shape[0] * CAP
    window, across_dft, down_dft = taper_and_dft()
    vmem = pl.BlockSpec(memory_space=pltpu.VMEM)
    return pl.pallas_call(
        grid_kernel,
        out_shape=jax.ShapeDtypeStruct((bands, SUB // bands, SG_DEV, LANES), jnp.float32),
        in_specs=[pl.BlockSpec(memory_space=pltpu.SMEM)] + [vmem] * 7,
        out_specs=vmem,
        scratch_shapes=[
            pltpu.VMEM((slots * SLOT_ROWS, LANES), jnp.float32),
            pltpu.VMEM((slots, 2 * VIS), jnp.float32),
            pltpu.VMEM((recv.shape[0], SUB, LANES), jnp.float32),
            pltpu.VMEM((SG_DEV, SUB, LANES), jnp.float32),
            pltpu.VMEM((12 * CHUNKS, 8, LANES), jnp.float32),
            pltpu.VMEM((4 * CHUNKS * 64, LANES), jnp.float32),
            pltpu.VMEM((12 * CHUNKS, 8, LANES), jnp.float32),
            pltpu.VMEM((4 * CHUNKS * 64, LANES), jnp.float32),
        ],
        compiler_params=pltpu.CompilerParams(vmem_limit_bytes=40 * 1024 * 1024),
        name="grid_blocks",
    )(
        tags,
        recv,
        other,
        scale,
        jnp.asarray(coordinate_spread(), jnp.bfloat16),
        jnp.asarray(window),
        jnp.asarray(across_dft),
        jnp.asarray(down_dft),
    )


def shards(visibility, weights, block_uv, chan_ratio, block_subgrid, block_stations, screens):
    grid_count = lax.axis_size("grid")
    bands = lax.axis_size("band")
    message = packed(
        visibility[0], weights[0], block_uv, block_subgrid, block_stations, screens[0], grid_count
    )
    recv = lax.all_to_all(message, "grid", split_axis=0, concat_axis=0, tiled=True)
    other = lax.ppermute(
        recv[:, CAP * SLOT_ROWS :], "grid", [(i, i ^ 1) for i in range(grid_count)]
    )
    first = 2 * 3 * TS
    tags = recv[:, : CAP * SLOT_ROWS].reshape(grid_count * CAP, SLOT_ROWS, LANES)[
        :, 2 * CHUNKS, first : first + 3
    ]
    tags = tags.astype(jnp.int32).reshape(-1)
    scale = jnp.tile(chan_ratio[0] * (math.pi / SUB), 2 * TS)[None, :]
    rows = gridded(tags, recv, other, scale, bands)
    parts = lax.all_to_all(rows, "band", split_axis=0, concat_axis=0, tiled=True)
    return jnp.sum(parts, axis=0)


def solution(mesh):
    in_specs = (
        P("band", "grid", None, None),
        P("band", "grid", None),
        P("grid", None, None),
        P("band", None),
        P("band", "grid"),
        P("grid", None),
        P("grid", None, None),
    )
    out_specs = P("band", "grid", None)
    return jax.shard_map(shards, mesh=mesh, in_specs=in_specs, out_specs=out_specs, check_vma=False)
```

```python
import math

import jax
import jax.numpy as jnp
import ml_dtypes
import numpy as np
from jax import lax
from jax.experimental import pallas as pl
from jax.experimental.pallas import tpu as pltpu
from jax.sharding import PartitionSpec as P

SUB = 64
TS = 16
CH = 24
VIS = TS * CH
SG_DEV = 8
CAP = 2
LANES = 128
CHUNKS = VIS // LANES
GROUPS_A_TURN = 8
SLOT_ROWS = 8
HALF_ROWS = SUB * SUB // 2 // LANES
MSG_ROWS = CAP * SLOT_ROWS + HALF_ROWS
PITCH = 264

ACROSS = np.array([a + s * (b + 0.5) for a in (-24, -8, 8, 24) for s in (1, -1) for b in range(8)])
DOWN_HALF = np.array([a + s * (b + 0.5) for a in (8, 24) for s in (1, -1) for b in range(8)])
DOWN = np.concatenate([DOWN_HALF, -DOWN_HALF])
PERM_X = (ACROSS + 31.5).astype(np.int64)
PERM_Y = (DOWN + 31.5).astype(np.int64)


def taper_and_dft():
    taper = np.sin(math.pi * (np.arange(SUB) + 0.5) / SUB)
    window = taper[PERM_Y][:, None] * taper[PERM_X][None, :] / VIS
    window = np.concatenate([window, window], axis=1)
    dft = np.exp(-2j * math.pi * np.outer(np.arange(SUB), np.arange(SUB)) / SUB) / math.sqrt(SUB)

    def real_form(perm):
        part = dft[:, perm].T
        form = np.block([[part.real, part.imag], [-part.imag, part.real]]).astype(np.float32)
        high = form.astype(ml_dtypes.bfloat16)
        low = (form - high.astype(np.float32)).astype(ml_dtypes.bfloat16)
        return np.concatenate([high, high, low], axis=0)

    return (
        window.astype(np.float32),
        real_form(PERM_X),
        real_form(PERM_Y),
    )


def coordinate_spread():
    spread = np.zeros((LANES, 2 * VIS), np.float32)
    for axis in range(2):
        for piece in range(3):
            for t in range(TS):
                spread[(piece * 2 + axis) * TS + t, axis * VIS + t * CH : axis * VIS + (t + 1) * CH] = 1.0
    return spread


def sincos(angle):
    square = angle * angle
    sine = angle * (
        0.999999987111644
        + square
        * (-0.16666619937913615 + square * (0.008330684107237122 + square * -0.00019359740077908407))
    )
    cosine = 0.999999999715393 + square * (
        -0.49999998388310446
        + square
        * (
            0.04166652058451844
            + square * (-0.0013884251197818648 + square * 2.4199524865236834e-05)
        )
    )
    return cosine, sine


def doubled(cosine, sine):
    twice = cosine + cosine
    return twice * cosine - 1.0, twice * sine


def half_steps(cosine, sine, cos_full):
    twice = cos_full + cos_full
    cos_list = [cosine, cosine * (twice - 1.0)]
    sin_list = [sine, sine * (twice + 1.0)]
    for _ in range(6):
        cos_list.append(twice * cos_list[-1] - cos_list[-2])
        sin_list.append(twice * sin_list[-1] - sin_list[-2])
    return cos_list, sin_list


def grid_kernel(
    tags,
    recv,
    other,
    scale,
    spread,
    window,
    across_dft,
    down_dft,
    out,
    rows,
    angles,
    beams,
    total,
    *buffers,
):
    sources = recv.shape[0]
    core = lax.rem(lax.axis_index("grid"), 2)
    lane = lax.broadcasted_iota(jnp.int32, (8, LANES), 1)
    low = lane < SUB

    def unpack(i, carry):
        rows[pl.ds(pl.multiple_of(i * 16, 16), 16), :] = recv[i, 0:16, :].astype(jnp.float32)
        mine = recv[i, 16:32, :].astype(jnp.float32)
        theirs = other[i].astype(jnp.float32)
        for half in range(2):
            part = jnp.where(core == half, mine, theirs)
            turned = pltpu.roll(part, SUB, 1)
            for j in range(2):
                a = part[8 * j : 8 * j + 8]
                b = turned[8 * j : 8 * j + 8]
                beams[i, half * 32 + j * 8 : half * 32 + j * 8 + 8, :] = jnp.where(low, a, b)
                beams[i, half * 32 + 16 + j * 8 : half * 32 + 16 + j * 8 + 8, :] = jnp.where(low, b, a)
        return carry

    lax.fori_loop(0, sources, unpack, 0, unroll=16)
    slots = sources * CAP
    coords = rows[pl.ds(6, slots, stride=SLOT_ROWS), :].astype(jnp.bfloat16)
    angles[...] = jnp.dot(coords, spread[...], preferred_element_type=jnp.float32) * scale[...]
    total[...] = jnp.zeros_like(total)
    sign = jnp.where(lax.broadcasted_iota(jnp.int32, (32, LANES), 1) < SUB, -1.0, 1.0)

    def anchor_row(part, chunk):
        return part * CHUNKS + chunk

    def base(g, anchors, steps):
        for c in range(CHUNKS):
            real = rows[pl.ds(g * 64 + c, 8, stride=SLOT_ROWS), :]
            imag = rows[pl.ds(g * 64 + CHUNKS + c, 8, stride=SLOT_ROWS), :]
            at = pl.ds(pl.multiple_of(g * 8, 8), 8)
            cu, su = sincos(angles[at, c * LANES : (c + 1) * LANES])
            cv, sv = sincos(angles[at, VIS + c * LANES : VIS + (c + 1) * LANES])
            cc = cu * cv - su * sv
            ss = su * cv + cu * sv
            xr = real * cc + imag * ss
            xi = imag * cc - real * ss
            for axis, (cosine, sine) in enumerate(((cu, su), (cv, sv))):
                c1, s1 = doubled(cosine, sine)
                cos_list, sin_list = half_steps(cosine, sine, c1)
                for b in range(8):
                    for part, value in ((2 * axis, cos_list[b]), (2 * axis + 1, sin_list[b])):
                        first = (part * CHUNKS + c) * 64 + b * 8
                        steps[first : first + 8, :] = value
                c8, s8 = doubled(*doubled(*doubled(c1, s1)))
                c16, s16 = doubled(c8, s8)
                twice = c8 + c8
                c24, s24 = twice * c16 - c8, twice * s16 - s8
                if axis == 0:
                    values = []
                    for ca, sa in ((c24, s24), (c8, s8)):
                        p, q, r, t = xr * ca, xi * sa, xr * sa, xi * ca
                        values.append(((p + q, t - r), (p - q, t + r)))
                    ordered = (values[0][0], values[1][0], values[1][1], values[0][1])
                    for a in range(4):
                        for k in range(2):
                            anchors[anchor_row(2 * a + k, c)] = ordered[a][k]
                else:
                    for a, pair in enumerate(((c8, s8), (c24, s24))):
                        for k in range(2):
                            anchors[anchor_row(8 + 2 * a + k, c)] = pair[k]

    def expand(g, anchors, steps):
        for s in range(8):

            def step(part, c):
                return steps[pl.ds((part * CHUNKS + c) * 64 + s, 8, stride=8), :]

            def anchor(part, c):
                return jnp.broadcast_to(anchors[anchor_row(part, c), s : s + 1, :], (8, LANES))

            left = [[None] * CHUNKS for _ in range(8)]
            right = [[None] * CHUNKS for _ in range(4)]
            for c in range(CHUNKS):
                d, e = step(0, c), step(1, c)
                for a in range(4):
                    pr, pi = anchor(2 * a, c), anchor(2 * a + 1, c)
                    rd, ie, re, id_ = pr * d, pi * e, pr * e, pi * d
                    left[a][c] = jnp.concatenate([rd - ie, rd + ie], axis=0).astype(jnp.bfloat16)
                    left[4 + a][c] = jnp.concatenate([id_ + re, id_ - re], axis=0).astype(jnp.bfloat16)
                d, e = step(2, c), step(3, c)
                for a in range(2):
                    ca, sa = anchor(8 + 2 * a, c), anchor(9 + 2 * a, c)
                    cd, se, sd, ce = ca * d, sa * e, sa * d, ca * e
                    right[a][c] = jnp.concatenate([cd, se], axis=0).astype(jnp.bfloat16)
                    right[2 + a][c] = jnp.concatenate([sd, ce], axis=0).astype(jnp.bfloat16)
            left_all = jnp.concatenate([jnp.concatenate(r, axis=1) for r in left], axis=0)
            right_all = jnp.concatenate([jnp.concatenate(r, axis=1) for r in right], axis=0)
            product = lax.dot_general(
                right_all, left_all, (((1,), (1,)), ((), ())), preferred_element_type=jnp.float32
            )
            q = [product[8 * j : 8 * j + 8] for j in range(8)]
            top = jnp.concatenate([q[0] - q[1], q[0] + q[1], q[2] - q[3], q[2] + q[3]], axis=0)
            bottom = jnp.concatenate([q[4] + q[5], q[4] - q[5], q[6] + q[7], q[6] - q[7]], axis=0)
            turned = pltpu.roll(bottom, SUB, 1) * sign
            image = jnp.concatenate([top + turned, top - turned], axis=0)
            slot = g * 8 + s
            target = tags[3 * slot]
            gain = beams[tags[3 * slot + 1]] * beams[tags[3 * slot + 2]]
            total[target] += gain * image

    turns = slots // 8 // GROUPS_A_TURN

    def turn(i, carry):
        for j in range(GROUPS_A_TURN):
            at = 2 * (j % 2)
            base(GROUPS_A_TURN * i + j, *buffers[at : at + 2])
            expand(GROUPS_A_TURN * i + j, *buffers[at : at + 2])
        return carry

    lax.fori_loop(0, turns, turn, 0)
    tapered = (total[...] * window[...]).reshape(SG_DEV * SUB, LANES)
    high, low_part = pieces_of(tapered)
    first = jnp.dot(
        jnp.concatenate([high, low_part, high], axis=1),
        across_dft[...],
        preferred_element_type=jnp.float32,
    )
    bands = out.shape[0]
    each = SUB // bands
    for g in range(SG_DEV):
        mine = first[g * SUB : (g + 1) * SUB]
        stacked = jnp.concatenate([mine[:, :SUB], mine[:, SUB:]], axis=0).T
        high, low_part = pieces_of(stacked)
        second = jnp.dot(
            jnp.concatenate([high, low_part, high], axis=1),
            down_dft[...],
            preferred_element_type=jnp.float32,
        )
        for b in range(bands):
            out[b, :, g, :] = second[b * each : (b + 1) * each]


def pieces_of(value):
    high = value.astype(jnp.bfloat16)
    return high, (value - high.astype(jnp.float32)).astype(jnp.bfloat16)


def pack_kernel(*refs):
    sources, out, placed, held, done = refs[:8], refs[8], refs[9], refs[10:18], refs[18]
    copies = [pltpu.make_async_copy(sources[i], held[i], done.at[i]) for i in range(8)]
    for copy in copies:
        copy.start()
    visibility, weights, coords, owned, stations, screen, turn_y, turn_x = held
    for copy in copies[2:]:
        copy.wait()
    blocks = weights.shape[0]
    dests = out.shape[0]
    lined = jnp.broadcast_to((owned[...] // SG_DEV).astype(jnp.float32), (blocks, blocks))
    first = lax.broadcasted_iota(jnp.int32, (blocks, blocks), 0)
    second = lax.broadcasted_iota(jnp.int32, (blocks, blocks), 1)
    earlier = jnp.where((lined.T == lined) & (first < second), 1.0, 0.0)
    rank = jnp.sum(earlier, axis=0, keepdims=True)
    dest = lax.broadcasted_iota(jnp.int32, (dests, blocks), 0).astype(jnp.float32)
    here = jnp.broadcast_to(lined[:1], (dests, blocks)) == dest
    ranks = jnp.broadcast_to(rank, (dests, blocks))
    choose = jnp.concatenate(
        [jnp.where(here & (ranks == k), 1.0, 0.0) for k in range(CAP)], axis=0
    ).astype(jnp.bfloat16)
    rest = coords[...]
    pieces = []
    for _ in range(3):
        pieces.append(rest.astype(jnp.bfloat16).astype(jnp.float32))
        rest = rest - pieces[-1]
    local = (owned[...] % SG_DEV).astype(jnp.float32)
    numbers = jnp.concatenate(
        [local, stations[...].astype(jnp.float32), jnp.zeros((5, blocks), jnp.float32)], axis=0
    )
    empty = jnp.zeros((LANES - 3 * coords.shape[0] - 8, blocks), jnp.float32)
    line = jnp.concatenate(pieces + [numbers, empty], axis=0).astype(jnp.bfloat16)
    at = 2 * CHUNKS * PITCH
    placed[at : at + CAP * dests, :] = lax.dot_general(
        choose, line, (((1,), (1,)), ((), ())), preferred_element_type=jnp.float32
    )
    at = (2 * CHUNKS + 1) * PITCH
    placed[at : at + CAP * dests, :] = jnp.zeros((CAP * dests, LANES), jnp.float32)
    turned = lax.dot_general(
        turn_y[...], screen[...], (((1,), (1,)), ((), ())), preferred_element_type=jnp.float32
    ).astype(jnp.bfloat16)
    halves = []
    for h in range(2):
        sides = [
            jnp.dot(
                turned[32 * h + 16 * k : 32 * h + 16 * k + 16],
                turn_x[k],
                preferred_element_type=jnp.float32,
            )
            for k in range(2)
        ]
        halves.append((sides[0] + sides[1]).astype(jnp.bfloat16))

    copies[1].wait()
    copies[0].wait()
    for c in range(CHUNKS):
        weight = weights[:, c * LANES : (c + 1) * LANES]
        for k in range(2):
            weighted = visibility[:, k, c * LANES : (c + 1) * LANES] * weight
            at = (k * CHUNKS + c) * PITCH
            placed[at : at + CAP * dests, :] = jnp.dot(
                choose, weighted.astype(jnp.bfloat16), preferred_element_type=jnp.float32
            )
    def write(i, carry):
        for h in range(2):
            d = 2 * i + h
            rows = [
                placed[pl.ds(k * dests + d, SLOT_ROWS, stride=PITCH), :] for k in range(CAP)
            ]
            out[d, 0 : CAP * SLOT_ROWS, :] = jnp.concatenate(rows, axis=0).astype(jnp.bfloat16)
            out[d, CAP * SLOT_ROWS :, :] = halves[h]
        return carry

    lax.fori_loop(0, dests // 2, write, 0, unroll=8)


def packed(visibility, weights, block_uv, targets, stations, screen, grid_count):
    blocks = visibility.shape[0]
    turn_y = np.zeros((SUB, SUB), np.float32)
    turn_y[np.arange(SUB), PERM_Y] = 1.0
    turn_x = np.zeros((2, SUB, LANES), np.float32)
    for k in range(2):
        turn_x[k, PERM_X, k * SUB + np.arange(SUB)] = 1.0
    operands = [
        visibility,
        weights,
        block_uv.transpose(1, 2, 0).reshape(2 * TS, blocks),
        targets,
        stations.T,
        screen,
        jnp.asarray(turn_y, jnp.bfloat16),
        jnp.asarray(turn_x, jnp.bfloat16),
    ]
    return pl.pallas_call(
        pack_kernel,
        out_shape=jax.ShapeDtypeStruct((grid_count, MSG_ROWS, LANES), jnp.bfloat16),
        in_specs=[pl.BlockSpec(memory_space=pltpu.HBM)] * 8,
        out_specs=pl.BlockSpec(memory_space=pltpu.VMEM),
        scratch_shapes=[pltpu.VMEM((SLOT_ROWS * PITCH, LANES), jnp.float32)]
        + [pltpu.VMEM(x.shape, x.dtype) for x in operands]
        + [pltpu.SemaphoreType.DMA((8,))],
        compiler_params=pltpu.CompilerParams(vmem_limit_bytes=56 * 1024 * 1024),
        name="pack_blocks",
    )(*operands)


def gridded(tags, recv, other, scale, bands):
    slots = recv.shape[0] * CAP
    window, across_dft, down_dft = taper_and_dft()
    vmem = pl.BlockSpec(memory_space=pltpu.VMEM)
    return pl.pallas_call(
        grid_kernel,
        out_shape=jax.ShapeDtypeStruct((bands, SUB // bands, SG_DEV, LANES), jnp.float32),
        in_specs=[pl.BlockSpec(memory_space=pltpu.SMEM)] + [vmem] * 7,
        out_specs=vmem,
        scratch_shapes=[
            pltpu.VMEM((slots * SLOT_ROWS, LANES), jnp.float32),
            pltpu.VMEM((slots, 2 * VIS), jnp.float32),
            pltpu.VMEM((recv.shape[0], SUB, LANES), jnp.float32),
            pltpu.VMEM((SG_DEV, SUB, LANES), jnp.float32),
            pltpu.VMEM((12 * CHUNKS, 8, LANES), jnp.float32),
            pltpu.VMEM((4 * CHUNKS * 64, LANES), jnp.float32),
            pltpu.VMEM((12 * CHUNKS, 8, LANES), jnp.float32),
            pltpu.VMEM((4 * CHUNKS * 64, LANES), jnp.float32),
        ],
        compiler_params=pltpu.CompilerParams(vmem_limit_bytes=40 * 1024 * 1024),
        name="grid_blocks",
    )(
        tags,
        recv,
        other,
        scale,
        jnp.asarray(coordinate_spread(), jnp.bfloat16),
        jnp.asarray(window),
        jnp.asarray(across_dft),
        jnp.asarray(down_dft),
    )


def shards(visibility, weights, block_uv, chan_ratio, block_subgrid, block_stations, screens):
    grid_count = lax.axis_size("grid")
    bands = lax.axis_size("band")
    message = packed(
        visibility[0], weights[0], block_uv, block_subgrid, block_stations, screens[0], grid_count
    )
    recv = lax.all_to_all(message, "grid", split_axis=0, concat_axis=0, tiled=True)
    other = lax.ppermute(
        recv[:, CAP * SLOT_ROWS :], "grid", [(i, i ^ 1) for i in range(grid_count)]
    )
    first = 2 * 3 * TS
    tags = recv[:, : CAP * SLOT_ROWS].reshape(grid_count * CAP, SLOT_ROWS, LANES)[
        :, 2 * CHUNKS, first : first + 3
    ]
    tags = tags.astype(jnp.int32).reshape(-1)
    scale = jnp.tile(chan_ratio[0] * (math.pi / SUB), 2 * TS)[None, :]
    rows = gridded(tags, recv, other, scale, bands)
    parts = lax.all_to_all(rows, "band", split_axis=0, concat_axis=0, tiled=True)
    return jnp.sum(parts, axis=0)


def solution(mesh):
    in_specs = (
        P("band", "grid", None, None),
        P("band", "grid", None),
        P("grid", None, None),
        P("band", None),
        P("band", "grid"),
        P("grid", None),
        P("grid", None, None),
    )
    out_specs = P("band", "grid", None)
    return jax.shard_map(shards, mesh=mesh, in_specs=in_specs, out_specs=out_specs, check_vma=False)
```

```python
import math

import jax
import jax.numpy as jnp
import ml_dtypes
import numpy as np
from jax import lax
from jax.experimental import pallas as pl
from jax.experimental.pallas import tpu as pltpu
from jax.sharding import PartitionSpec as P

SUB = 64
TS = 16
CH = 24
VIS = TS * CH
SG_DEV = 8
CAP = 2
LANES = 128
CHUNKS = VIS // LANES
GROUPS_A_TURN = 8
SLOT_ROWS = 8
HALF_ROWS = SUB * SUB // 2 // LANES
MSG_ROWS = CAP * SLOT_ROWS + HALF_ROWS
PITCH = 264

ACROSS = np.array([a + s * (b + 0.5) for a in (-24, -8, 8, 24) for s in (1, -1) for b in range(8)])
DOWN_HALF = np.array([a + s * (b + 0.5) for a in (8, 24) for s in (1, -1) for b in range(8)])
DOWN = np.concatenate([DOWN_HALF, -DOWN_HALF])
PERM_X = (ACROSS + 31.5).astype(np.int64)
PERM_Y = (DOWN + 31.5).astype(np.int64)


def taper_and_dft():
    taper = np.sin(math.pi * (np.arange(SUB) + 0.5) / SUB)
    window = taper[PERM_Y][:, None] * taper[PERM_X][None, :] / VIS
    window = np.concatenate([window, window], axis=1)
    dft = np.exp(-2j * math.pi * np.outer(np.arange(SUB), np.arange(SUB)) / SUB) / math.sqrt(SUB)

    def real_form(perm):
        part = dft[:, perm].T
        form = np.block([[part.real, part.imag], [-part.imag, part.real]]).astype(np.float32)
        high = form.astype(ml_dtypes.bfloat16)
        low = (form - high.astype(np.float32)).astype(ml_dtypes.bfloat16)
        return np.concatenate([high, high, low], axis=0)

    return (
        window.astype(np.float32),
        real_form(PERM_X),
        real_form(PERM_Y),
    )


def coordinate_spread():
    spread = np.zeros((LANES, 2 * VIS), np.float32)
    for axis in range(2):
        for piece in range(3):
            for t in range(TS):
                spread[(piece * 2 + axis) * TS + t, axis * VIS + t * CH : axis * VIS + (t + 1) * CH] = 1.0
    return spread


def sincos(angle):
    square = angle * angle
    sine = angle * (
        0.999999987111644
        + square
        * (-0.16666619937913615 + square * (0.008330684107237122 + square * -0.00019359740077908407))
    )
    cosine = 0.999999999715393 + square * (
        -0.49999998388310446
        + square
        * (
            0.04166652058451844
            + square * (-0.0013884251197818648 + square * 2.4199524865236834e-05)
        )
    )
    return cosine, sine


def doubled(cosine, sine):
    twice = cosine + cosine
    return twice * cosine - 1.0, twice * sine


def half_steps(cosine, sine, cos_full):
    twice = cos_full + cos_full
    cos_list = [cosine, cosine * (twice - 1.0)]
    sin_list = [sine, sine * (twice + 1.0)]
    for _ in range(6):
        cos_list.append(twice * cos_list[-1] - cos_list[-2])
        sin_list.append(twice * sin_list[-1] - sin_list[-2])
    return cos_list, sin_list


def grid_kernel(
    tags,
    recv,
    other,
    scale,
    spread,
    window,
    across_dft,
    down_dft,
    out,
    rows,
    angles,
    beams,
    total,
    ordered_rows,
    *buffers,
):
    sources = recv.shape[0]
    core = lax.rem(lax.axis_index("grid"), 2)
    lane = lax.broadcasted_iota(jnp.int32, (8, LANES), 1)
    low = lane < SUB

    def unpack(i, carry):
        rows[pl.ds(pl.multiple_of(i * 16, 16), 16), :] = recv[i, 0:16, :].astype(jnp.float32)
        mine = recv[i, 16:32, :].astype(jnp.float32)
        theirs = other[i].astype(jnp.float32)
        for half in range(2):
            part = jnp.where(core == half, mine, theirs)
            turned = pltpu.roll(part, SUB, 1)
            for j in range(2):
                a = part[8 * j : 8 * j + 8]
                b = turned[8 * j : 8 * j + 8]
                beams[i, half * 32 + j * 8 : half * 32 + j * 8 + 8, :] = jnp.where(low, a, b)
                beams[i, half * 32 + 16 + j * 8 : half * 32 + 16 + j * 8 + 8, :] = jnp.where(low, b, a)
        return carry

    lax.fori_loop(0, sources, unpack, 0, unroll=16)
    slots = sources * CAP
    coords = rows[pl.ds(6, slots, stride=SLOT_ROWS), :].astype(jnp.bfloat16)
    angles[...] = jnp.dot(coords, spread[...], preferred_element_type=jnp.float32) * scale[...]
    total[...] = jnp.zeros_like(total)
    sign = jnp.where(lax.broadcasted_iota(jnp.int32, (32, LANES), 1) < SUB, -1.0, 1.0)

    def anchor_row(part, chunk):
        return part * CHUNKS + chunk

    def base(g, anchors, steps):
        for c in range(CHUNKS):
            real = rows[pl.ds(g * 64 + c, 8, stride=SLOT_ROWS), :]
            imag = rows[pl.ds(g * 64 + CHUNKS + c, 8, stride=SLOT_ROWS), :]
            at = pl.ds(pl.multiple_of(g * 8, 8), 8)
            cu, su = sincos(angles[at, c * LANES : (c + 1) * LANES])
            cv, sv = sincos(angles[at, VIS + c * LANES : VIS + (c + 1) * LANES])
            cc = cu * cv - su * sv
            ss = su * cv + cu * sv
            xr = real * cc + imag * ss
            xi = imag * cc - real * ss
            for axis, (cosine, sine) in enumerate(((cu, su), (cv, sv))):
                c1, s1 = doubled(cosine, sine)
                cos_list, sin_list = half_steps(cosine, sine, c1)
                for b in range(8):
                    for part, value in ((2 * axis, cos_list[b]), (2 * axis + 1, sin_list[b])):
                        first = (part * CHUNKS + c) * 64 + b * 8
                        steps[first : first + 8, :] = value
                c8, s8 = doubled(*doubled(*doubled(c1, s1)))
                c16, s16 = doubled(c8, s8)
                twice = c8 + c8
                c24, s24 = twice * c16 - c8, twice * s16 - s8
                if axis == 0:
                    values = []
                    for ca, sa in ((c24, s24), (c8, s8)):
                        p, q, r, t = xr * ca, xi * sa, xr * sa, xi * ca
                        values.append(((p + q, t - r), (p - q, t + r)))
                    ordered = (values[0][0], values[1][0], values[1][1], values[0][1])
                    for a in range(4):
                        for k in range(2):
                            anchors[anchor_row(2 * a + k, c)] = ordered[a][k]
                else:
                    for a, pair in enumerate(((c8, s8), (c24, s24))):
                        for k in range(2):
                            anchors[anchor_row(8 + 2 * a + k, c)] = pair[k]

    def expand(g, anchors, steps):
        for s in range(8):

            def step(part, c):
                return steps[pl.ds((part * CHUNKS + c) * 64 + s, 8, stride=8), :]

            def anchor(part, c):
                return jnp.broadcast_to(anchors[anchor_row(part, c), s : s + 1, :], (8, LANES))

            left = [[None] * CHUNKS for _ in range(8)]
            right = [[None] * CHUNKS for _ in range(4)]
            for c in range(CHUNKS):
                d, e = step(0, c), step(1, c)
                for a in range(4):
                    pr, pi = anchor(2 * a, c), anchor(2 * a + 1, c)
                    rd, ie, re, id_ = pr * d, pi * e, pr * e, pi * d
                    left[a][c] = jnp.concatenate([rd - ie, rd + ie], axis=0).astype(jnp.bfloat16)
                    left[4 + a][c] = jnp.concatenate([id_ + re, id_ - re], axis=0).astype(jnp.bfloat16)
                d, e = step(2, c), step(3, c)
                for a in range(2):
                    ca, sa = anchor(8 + 2 * a, c), anchor(9 + 2 * a, c)
                    cd, se, sd, ce = ca * d, sa * e, sa * d, ca * e
                    right[a][c] = jnp.concatenate([cd, se], axis=0).astype(jnp.bfloat16)
                    right[2 + a][c] = jnp.concatenate([sd, ce], axis=0).astype(jnp.bfloat16)
            left_all = jnp.concatenate([jnp.concatenate(r, axis=1) for r in left], axis=0)
            right_all = jnp.concatenate([jnp.concatenate(r, axis=1) for r in right], axis=0)
            product = lax.dot_general(
                right_all, left_all, (((1,), (1,)), ((), ())), preferred_element_type=jnp.float32
            )
            q = [product[8 * j : 8 * j + 8] for j in range(8)]
            top = jnp.concatenate([q[0] - q[1], q[0] + q[1], q[2] - q[3], q[2] + q[3]], axis=0)
            bottom = jnp.concatenate([q[4] + q[5], q[4] - q[5], q[6] + q[7], q[6] - q[7]], axis=0)
            turned = pltpu.roll(bottom, SUB, 1) * sign
            image = jnp.concatenate([top + turned, top - turned], axis=0)
            slot = g * 8 + s
            target = tags[3 * slot]
            gain = beams[tags[3 * slot + 1]] * beams[tags[3 * slot + 2]]
            total[target] += gain * image

    turns = slots // 8 // GROUPS_A_TURN

    def turn(i, carry):
        for j in range(GROUPS_A_TURN):
            at = 2 * (j % 2)
            base(GROUPS_A_TURN * i + j, *buffers[at : at + 2])
            expand(GROUPS_A_TURN * i + j, *buffers[at : at + 2])
        return carry

    lax.fori_loop(0, turns, turn, 0)
    tapered = (total[...] * window[...]).reshape(SG_DEV * SUB, LANES)
    high, low_part = pieces_of(tapered)
    first = jnp.dot(
        jnp.concatenate([high, low_part, high], axis=1),
        across_dft[...],
        preferred_element_type=jnp.float32,
    )
    for g in range(SG_DEV):
        mine = first[g * SUB : (g + 1) * SUB]
        stacked = jnp.concatenate([mine[:, :SUB], mine[:, SUB:]], axis=0).T
        high, low_part = pieces_of(stacked)
        second = jnp.dot(
            jnp.concatenate([high, low_part, high], axis=1),
            down_dft[...],
            preferred_element_type=jnp.float32,
        )
        ordered_rows[:, g, :] = second
    out[...] = ordered_rows[...].reshape(out.shape).astype(out.dtype)


def pieces_of(value):
    high = value.astype(jnp.bfloat16)
    return high, (value - high.astype(jnp.float32)).astype(jnp.bfloat16)


def pack_kernel(*refs):
    sources, out, placed, held, done = refs[:8], refs[8], refs[9], refs[10:18], refs[18]
    copies = [pltpu.make_async_copy(sources[i], held[i], done.at[i]) for i in range(8)]
    for copy in copies:
        copy.start()
    visibility, weights, coords, owned, stations, screen, turn_y, turn_x = held
    for copy in copies[2:]:
        copy.wait()
    blocks = weights.shape[0]
    dests = out.shape[0]
    lined = jnp.broadcast_to((owned[...] // SG_DEV).astype(jnp.float32), (blocks, blocks))
    first = lax.broadcasted_iota(jnp.int32, (blocks, blocks), 0)
    second = lax.broadcasted_iota(jnp.int32, (blocks, blocks), 1)
    earlier = jnp.where((lined.T == lined) & (first < second), 1.0, 0.0)
    rank = jnp.sum(earlier, axis=0, keepdims=True)
    dest = lax.broadcasted_iota(jnp.int32, (dests, blocks), 0).astype(jnp.float32)
    here = jnp.broadcast_to(lined[:1], (dests, blocks)) == dest
    ranks = jnp.broadcast_to(rank, (dests, blocks))
    choose = jnp.concatenate(
        [jnp.where(here & (ranks == k), 1.0, 0.0) for k in range(CAP)], axis=0
    ).astype(jnp.bfloat16)
    rest = coords[...]
    pieces = []
    for _ in range(3):
        pieces.append(rest.astype(jnp.bfloat16).astype(jnp.float32))
        rest = rest - pieces[-1]
    local = (owned[...] % SG_DEV).astype(jnp.float32)
    numbers = jnp.concatenate(
        [local, stations[...].astype(jnp.float32), jnp.zeros((5, blocks), jnp.float32)], axis=0
    )
    empty = jnp.zeros((LANES - 3 * coords.shape[0] - 8, blocks), jnp.float32)
    line = jnp.concatenate(pieces + [numbers, empty], axis=0).astype(jnp.bfloat16)
    at = 2 * CHUNKS * PITCH
    placed[at : at + CAP * dests, :] = lax.dot_general(
        choose, line, (((1,), (1,)), ((), ())), preferred_element_type=jnp.float32
    )
    at = (2 * CHUNKS + 1) * PITCH
    placed[at : at + CAP * dests, :] = jnp.zeros((CAP * dests, LANES), jnp.float32)
    turned = lax.dot_general(
        turn_y[...], screen[...], (((1,), (1,)), ((), ())), preferred_element_type=jnp.float32
    ).astype(jnp.bfloat16)
    halves = []
    for h in range(2):
        sides = [
            jnp.dot(
                turned[32 * h + 16 * k : 32 * h + 16 * k + 16],
                turn_x[k],
                preferred_element_type=jnp.float32,
            )
            for k in range(2)
        ]
        halves.append((sides[0] + sides[1]).astype(jnp.bfloat16))

    copies[1].wait()
    copies[0].wait()
    for c in range(CHUNKS):
        weight = weights[:, c * LANES : (c + 1) * LANES]
        for k in range(2):
            weighted = visibility[:, k, c * LANES : (c + 1) * LANES] * weight
            at = (k * CHUNKS + c) * PITCH
            placed[at : at + CAP * dests, :] = jnp.dot(
                choose, weighted.astype(jnp.bfloat16), preferred_element_type=jnp.float32
            )
    def write(i, carry):
        for h in range(2):
            d = 2 * i + h
            rows = [
                placed[pl.ds(k * dests + d, SLOT_ROWS, stride=PITCH), :] for k in range(CAP)
            ]
            out[d, 0 : CAP * SLOT_ROWS, :] = jnp.concatenate(rows, axis=0).astype(jnp.bfloat16)
            out[d, CAP * SLOT_ROWS :, :] = halves[h]
        return carry

    lax.fori_loop(0, dests // 2, write, 0, unroll=8)


def packed(visibility, weights, block_uv, targets, stations, screen, grid_count):
    blocks = visibility.shape[0]
    turn_y = np.zeros((SUB, SUB), np.float32)
    turn_y[np.arange(SUB), PERM_Y] = 1.0
    turn_x = np.zeros((2, SUB, LANES), np.float32)
    for k in range(2):
        turn_x[k, PERM_X, k * SUB + np.arange(SUB)] = 1.0
    operands = [
        visibility,
        weights,
        block_uv.transpose(1, 2, 0).reshape(2 * TS, blocks),
        targets,
        stations.T,
        screen,
        jnp.asarray(turn_y, jnp.bfloat16),
        jnp.asarray(turn_x, jnp.bfloat16),
    ]
    return pl.pallas_call(
        pack_kernel,
        out_shape=jax.ShapeDtypeStruct((grid_count, MSG_ROWS, LANES), jnp.bfloat16),
        in_specs=[pl.BlockSpec(memory_space=pltpu.HBM)] * 8,
        out_specs=pl.BlockSpec(memory_space=pltpu.VMEM),
        scratch_shapes=[pltpu.VMEM((SLOT_ROWS * PITCH, LANES), jnp.float32)]
        + [pltpu.VMEM(x.shape, x.dtype) for x in operands]
        + [pltpu.SemaphoreType.DMA((8,))],
        compiler_params=pltpu.CompilerParams(vmem_limit_bytes=56 * 1024 * 1024),
        name="pack_blocks",
    )(*operands)


def gridded(tags, recv, other, scale, bands):
    slots = recv.shape[0] * CAP
    window, across_dft, down_dft = taper_and_dft()
    vmem = pl.BlockSpec(memory_space=pltpu.VMEM)
    return pl.pallas_call(
        grid_kernel,
        out_shape=jax.ShapeDtypeStruct((bands, SUB // bands * SG_DEV, LANES), jnp.bfloat16),
        in_specs=[pl.BlockSpec(memory_space=pltpu.SMEM)] + [vmem] * 7,
        out_specs=vmem,
        scratch_shapes=[
            pltpu.VMEM((slots * SLOT_ROWS, LANES), jnp.float32),
            pltpu.VMEM((slots, 2 * VIS), jnp.float32),
            pltpu.VMEM((recv.shape[0], SUB, LANES), jnp.float32),
            pltpu.VMEM((SG_DEV, SUB, LANES), jnp.float32),
            pltpu.VMEM((SUB, SG_DEV, LANES), jnp.float32),
            pltpu.VMEM((12 * CHUNKS, 8, LANES), jnp.float32),
            pltpu.VMEM((4 * CHUNKS * 64, LANES), jnp.float32),
            pltpu.VMEM((12 * CHUNKS, 8, LANES), jnp.float32),
            pltpu.VMEM((4 * CHUNKS * 64, LANES), jnp.float32),
        ],
        compiler_params=pltpu.CompilerParams(vmem_limit_bytes=40 * 1024 * 1024),
        name="grid_blocks",
    )(
        tags,
        recv,
        other,
        scale,
        jnp.asarray(coordinate_spread(), jnp.bfloat16),
        jnp.asarray(window),
        jnp.asarray(across_dft),
        jnp.asarray(down_dft),
    )


def shards(visibility, weights, block_uv, chan_ratio, block_subgrid, block_stations, screens):
    grid_count = lax.axis_size("grid")
    bands = lax.axis_size("band")
    message = packed(
        visibility[0], weights[0], block_uv, block_subgrid, block_stations, screens[0], grid_count
    )
    recv = lax.all_to_all(message, "grid", split_axis=0, concat_axis=0, tiled=True)
    other = lax.ppermute(
        recv[:, CAP * SLOT_ROWS :], "grid", [(i, i ^ 1) for i in range(grid_count)]
    )
    first = 2 * 3 * TS
    tags = recv[:, : CAP * SLOT_ROWS].reshape(grid_count * CAP, SLOT_ROWS, LANES)[
        :, 2 * CHUNKS, first : first + 3
    ]
    tags = tags.astype(jnp.int32).reshape(-1)
    scale = jnp.tile(chan_ratio[0] * (math.pi / SUB), 2 * TS)[None, :]
    rows = gridded(tags, recv, other, scale, bands)
    parts = lax.all_to_all(rows, "band", split_axis=0, concat_axis=0, tiled=True)
    total = jnp.sum(parts.astype(jnp.float32), axis=0)
    return total.reshape(SUB // bands, SG_DEV, LANES)


def solution(mesh):
    in_specs = (
        P("band", "grid", None, None),
        P("band", "grid", None),
        P("grid", None, None),
        P("band", None),
        P("band", "grid"),
        P("grid", None),
        P("grid", None, None),
    )
    out_specs = P("band", "grid", None)
    return jax.shard_map(shards, mesh=mesh, in_specs=in_specs, out_specs=out_specs, check_vma=False)
```
